32 devices in a mesh: qpt: 2 (over x), grow: 16 (over z, y, core).
Axes of the slice: x: 2, y: 2, z: 4, core: 2. Of those that a mesh axis runs over, the one named last changes fastest.
Arguments:
- pair_values: bfloat16 [2048, 8192], P('qpt', 'grow'), parts along dimension 0, may hold values from -4 to 4
- pair_scales: float32 [256, 2048], P('grow', 'qpt'), parts along dimension 1, may hold values from 0.2 to 2
- valence_index: int32 [2048], P('qpt'), parts along dimension 0, may hold values from 0 to 2047
- conduction_index: int32 [2048], P('qpt'), parts along dimension 0, may hold values from 0 to 2047
- valence_energy: float32 [2048], replicated, may hold values from -12 to -0.5
- conduction_energy: float32 [2048], replicated, may hold values from 0.5 to 15
- frequencies: float32 [2], replicated, may hold values from 0.5 to 5
- g_order: int32 [8192], replicated, may hold values from 0 to 8191, each once
Outputs:
- chi_zero: float32 [2, 16384, 8192], P(None, ('qpt', 'grow')), parts along dimension 1
The draws below stay inside these ranges and needn't reach their ends.
There are 2 independent parts, one for each index of `qpt`. The reference program is written for one: setup_inputs(seed, part) draws one part's arguments, and reference() takes and returns one part's arrays. A program takes and returns all parts, laid end to end along the dimension named above; an argument that names none is the same for every part. Nothing has to cross between parts.
Inputs may be any that keep to these rules, and one draw needn't show every extreme that they name: `g_order`: each G-vector appears exactly once.
All inputs are finite; a program needn't handle non-finite values.
Results may differ from the reference program's by a relative error of at most 0.0085.
Values may be sent and summed in bfloat16 or wider, within the bound.
A program may use at most 192 MiB of HBM per device.

```python
import math
import jax
import jax.numpy as jnp
from jax import lax

PAIRS = 1024
NG = 8192
NV = 2048
NC = 2048
NW = 2
GB = 32


def place_ends(array, own_key, low, largest):
    place = [jax.random.randint(jax.random.fold_in(own_key, axis), (), 0, length) for axis, length in enumerate(array.shape)]
    longest = array.shape.index(max(array.shape))
    beside = place[:longest] + [(place[longest] + 1) % array.shape[longest]] + place[longest + 1:]
    return array.at[tuple(place)].set(low).at[tuple(beside)].set(largest)


def level_of(stream_key, extent, split, least, largest):
    factor_of, own = 1.0, jax.random.fold_in(stream_key, 6)
    for axis_at, shards_of in split:
        draws = jnp.exp(jax.random.uniform(jax.random.fold_in(own, axis_at), (shards_of,), jnp.float32, least / len(split), largest / len(split)))
        factor_of = factor_of * jnp.repeat(draws, extent[axis_at] // shards_of).reshape([-1 if axis == axis_at else 1 for axis in range(len(extent))])
    return factor_of


def gaussian(key, extent, deviation, most, cuts=(), kind=jnp.bfloat16):
    values = deviation * jax.random.normal(key, extent, jnp.float32)
    if cuts:
        values = values * level_of(key, extent, cuts, -0.22, 0.18)
    return jnp.clip(values, -most, most).astype(kind)


def setup_inputs(seed: int = 0, part: int = 0) -> dict:
    key_of = jax.random.split(jax.random.key(seed), 9)
    part_keys = jax.random.split(jax.random.fold_in(key_of[8], part), 9)
    return {
        "pair_values": gaussian(part_keys[0], (PAIRS, NG), 1.0, 4.0, ((1, 16),)),
        "pair_scales": jnp.clip(jnp.exp(math.log(2.0) - 2.3025851 * jax.random.uniform(part_keys[1], (NG // GB, PAIRS), jnp.float32) ** level_of(part_keys[1], (NG // GB, PAIRS), ((0, 16),), -0.2, 0.2)), 0.2, 2.0),
        "valence_index": place_ends(jax.random.randint(part_keys[2], (PAIRS,), 0, NV), jax.random.fold_in(part_keys[2], 1), 0, NV - 1).astype(jnp.int32),
        "conduction_index": place_ends(jax.random.randint(part_keys[3], (PAIRS,), 0, NC), jax.random.fold_in(part_keys[3], 1), 0, NC - 1).astype(jnp.int32),
        "valence_energy": jnp.clip(jax.random.uniform(key_of[4], (NV,), jnp.float32, -12.0, -0.5), -12.0, -0.5),
        "conduction_energy": jnp.clip(jax.random.uniform(key_of[5], (NC,), jnp.float32, 0.5, 15.0), 0.5, 15.0),
        "frequencies": jnp.clip(jnp.exp(jax.random.uniform(key_of[6], (NW,), jnp.float32, math.log(0.5), math.log(5.0))), 0.5, 5.0),
        "g_order": jax.random.permutation(key_of[7], NG).astype(jnp.int32),
    }


def lookup_level(levels, index):
    onehot = (index[:, None] == jnp.arange(levels.shape[0], dtype=jnp.int32)[None, :]).astype(jnp.float32)
    return jnp.dot(onehot, levels, precision=lax.Precision.HIGHEST)


def pair_weights(valence_index, conduction_index, valence_energy, conduction_energy, frequencies):
    energy_gap = lookup_level(valence_energy, valence_index) - lookup_level(conduction_energy, conduction_index)
    denominator = 2.0 * energy_gap[:, None] / (energy_gap[:, None] ** 2 + frequencies[None, :] ** 2)
    return denominator * (float(valence_index.shape[0]) ** -0.5)


def dequantize(values, scales, block):
    factor = jnp.repeat(scales.T, block, axis=1)
    return (values.astype(jnp.float32) * factor).astype(jnp.bfloat16)


def reference(pair_values, pair_scales, valence_index, conduction_index, valence_energy, conduction_energy, frequencies, g_order):
    weights = pair_weights(valence_index, conduction_index, valence_energy, conduction_energy, frequencies)
    dense = dequantize(pair_values, pair_scales, GB)
    inverse = jnp.argsort(g_order).astype(jnp.int32)
    natural = jnp.take(dense, inverse, axis=1)
    results = []
    for freq_slot in range(NW):
        scaled = (weights[:, freq_slot:freq_slot + 1] * dense.astype(jnp.float32)).astype(jnp.bfloat16)
        results.append(jnp.dot(scaled.T, natural, preferred_element_type=jnp.float32))
    return jnp.stack(results)
```

```python
import functools

import jax
import jax.numpy as jnp
from jax import lax
from jax.experimental import pallas as pl
from jax.experimental.pallas import tpu as pltpu
from jax.sharding import PartitionSpec as P

LANES = 128
MESH = pl.DeviceIdType.MESH


def lookup_level(levels, index):
    hit = jnp.arange(levels.shape[0], dtype=jnp.int32)[:, None] == index[None, :]
    return jnp.sum(jnp.where(hit, levels[:, None], 0.0), axis=0)


def pair_weights(valence_index, conduction_index, valence_energy, conduction_energy, frequencies):
    energy_gap = lookup_level(valence_energy, valence_index) - lookup_level(
        conduction_energy, conduction_index
    )
    denominator = 2.0 * energy_gap[None, :] / (energy_gap[None, :] ** 2 + frequencies[:, None] ** 2)
    return denominator * float(valence_index.shape[0]) ** (-0.5)


def piece_table(tile_rows, group, across):
    if tile_rows % 128 or tile_rows < 512:
        return [(0, tile_rows * group, False)]
    early = tile_rows // 8 if across > 1 else 0
    part = (tile_rows - early) // 4
    cuts = [(k * part * group, part * group, False) for k in range(4)]
    if early:
        cuts.insert(0, (4 * part * group, early * group, True))
    return cuts


def gather_kernel(deep, across, pieces, x_ref, out_ref, send_sem, recv_sem, own_sem):
    count = len(pieces)
    block_rows = x_ref.shape[0]
    total = deep * across * 2
    q = lax.axis_index("qpt")
    me = lax.axis_index("grow")
    z = me // (2 * across)
    y = (me // 2) % across
    core = me % 2

    def place(zz, yy, cc):
        return (zz * across + yy) * 2 + cc

    beside = place(z, y, 1 - core)
    over = place(z, (across - 1) - y, core)
    up, down = place(z + 1, y, core), place(z - 1, y, core)
    has_up, has_down = z < deep - 1, z > 0

    barrier = pltpu.get_barrier_semaphore()
    pl.semaphore_signal(barrier, inc=1, device_id=(q, beside), device_id_type=MESH)
    if across > 1:
        pl.semaphore_signal(barrier, inc=1, device_id=(q, over), device_id_type=MESH)

    @pl.when(has_up)
    def _():
        pl.semaphore_signal(barrier, inc=1, device_id=(q, up), device_id_type=MESH)

    @pl.when(has_down)
    def _():
        pl.semaphore_signal(barrier, inc=1, device_id=(q, down), device_id_type=MESH)

    pl.semaphore_wait(
        barrier,
        1 + (across > 1) + has_up.astype(jnp.int32) + has_down.astype(jnp.int32),
    )

    def copy(kind, owner, j, target, own):
        first, rows, _ = pieces[j]
        landing = out_ref.at[pl.ds(pl.multiple_of(owner * block_rows + first, 16), rows), :]
        source = x_ref.at[pl.ds(first, rows), :] if own else landing
        slot = owner * count + j
        return pltpu.make_async_remote_copy(
            src_ref=source,
            dst_ref=landing,
            send_sem=send_sem.at[kind * (total * count) + slot],
            recv_sem=recv_sem.at[slot],
            device_id=(q, target),
            device_id_type=MESH,
        )

    def arrive(owner, j):
        copy(0, owner, j, beside, False).wait_recv()

    def pass_on(owner, j, came, same_y, act):
        own = came == 0 and same_y
        early = pieces[j][2]
        along_z = same_y or early
        if along_z and came >= 0:

            @pl.when(has_up)
            def _():
                act(copy(0, owner, j, up, own))

        if along_z and came <= 0:

            @pl.when(has_down)
            def _():
                act(copy(1, owner, j, down, own))

        if across > 1 and same_y and (not early or came == 0):
            act(copy(2, owner, j, over, own))
        act(copy(3, owner, j, beside, own))

    def steps():
        for r in range(1, deep + 1):
            for j in range(count):
                yield r, j

    def visit_half(step, j, same_y, arrived, act):
        yy = y if same_y else (across - 1) - y
        if step == 0:
            owner = place(z, yy, core)
            if arrived and not same_y:
                arrive(owner, j)
            pass_on(owner, j, 0, same_y, act)
            return
        for came in (1, -1):
            near = z - came * step
            inside = (near >= 0) if came == 1 else (near < deep)

            @pl.when(inside)
            def _():
                owner = place(near, yy, core)
                if arrived:
                    arrive(owner, j)
                pass_on(owner, j, came, same_y, act)

    def start(c):
        c.start()

    def left(c):
        c.wait_send()

    own_copy = pltpu.make_async_copy(
        x_ref, out_ref.at[pl.ds(pl.multiple_of(me * block_rows, 16), block_rows), :], own_sem
    )
    for j in range(count):
        visit_half(0, j, True, True, start)
    own_copy.start()
    for r, j in steps():
        if r < deep:
            visit_half(r, j, True, True, start)
        if across > 1:
            visit_half(r - 1, j, False, True, start)
    for zz in range(deep):
        for yy in range(across):
            for j in range(count):
                arrive(place(zz, yy, 1 - core), j)
    own_copy.wait()
    for r in range(deep):
        for j in range(count):
            visit_half(r, j, True, False, left)
            if across > 1:
                visit_half(r, j, False, False, left)


def gather_rows(block, total, qpt):
    group = 8
    across = max(1, min(4 // max(qpt, 1), total // 2))
    deep = total // (2 * across)
    pieces = piece_table(block.shape[0] // group, group, across)
    return pl.pallas_call(
        functools.partial(gather_kernel, deep, across, pieces),
        out_shape=jax.ShapeDtypeStruct((total * block.shape[0], LANES), block.dtype),
        in_specs=[pl.BlockSpec(memory_space=pl.ANY)],
        out_specs=pl.BlockSpec(memory_space=pl.ANY),
        scratch_shapes=[
            pltpu.SemaphoreType.DMA((4 * total * len(pieces),)),
            pltpu.SemaphoreType.DMA((total * len(pieces),)),
            pltpu.SemaphoreType.DMA,
        ],
        compiler_params=pltpu.CompilerParams(collective_id=0, has_side_effects=True),
    )(block)


def product_kernel(sources, group, wide, order_ref, src_ref, left_ref, out_ref, natural):
    step = pl.program_id(0)

    @pl.when(step < sources)
    def _():
        pairs = src_ref.shape[0] // (2 * group)

        def place(i, carry):
            rows = src_ref[pl.ds(pl.multiple_of(i * 2 * group, 2 * group), 2 * group), :].astype(
                jnp.float32
            )
            base = step * (2 * pairs) + 2 * i
            for half in range(2):
                g = order_ref[base + half]
                natural[pl.ds(pl.multiple_of(g * group, group), group), :] = rows[
                    half * group : (half + 1) * group
                ]
            return carry

        lax.fori_loop(0, pairs, place, 0, unroll=16)

    @pl.when(step >= sources)
    def _():
        first = (step - sources) * (wide * group)
        right = jnp.concatenate(
            [
                natural[pl.ds(first + k, wide, stride=group), :].astype(jnp.bfloat16)
                for k in range(group)
            ],
            axis=1,
        )
        freq_count, tile_rows, pair_count = left_ref.shape
        for w in range(freq_count):
            out_ref[w] = lax.dot_general(
                left_ref[w], right, (((1,), (1,)), ((), ())), preferred_element_type=jnp.float32
            )


def ordered_product(left, gathered, g_order, sources):
    freq_count, tile_rows, pair_count = left.shape
    total_cols = g_order.shape[0]
    group = pair_count // LANES
    wide = 512
    tiles = total_cols // wide
    chunk = gathered.shape[0] // sources
    return pl.pallas_call(
        functools.partial(product_kernel, sources, group, wide),
        out_shape=jax.ShapeDtypeStruct((freq_count, tile_rows, total_cols), jnp.float32),
        grid_spec=pltpu.PrefetchScalarGridSpec(
            num_scalar_prefetch=1,
            grid=(sources + tiles,),
            in_specs=[
                pl.BlockSpec((chunk, LANES), lambda i, order: (jnp.minimum(i, sources - 1), 0)),
                pl.BlockSpec((freq_count, tile_rows, pair_count), lambda i, order: (0, 0, 0)),
            ],
            out_specs=pl.BlockSpec(
                (freq_count, tile_rows, wide),
                lambda i, order: (0, 0, jnp.maximum(i - sources, 0)),
            ),
            scratch_shapes=[pltpu.VMEM((total_cols * group, LANES), jnp.float32)],
        ),
        compiler_params=pltpu.CompilerParams(
            dimension_semantics=("arbitrary",), vmem_limit_bytes=56 * 1024 * 1024
        ),
        cost_estimate=pl.CostEstimate(
            flops=2 * freq_count * tile_rows * total_cols * pair_count,
            bytes_accessed=freq_count * tile_rows * total_cols * 4,
            transcendentals=0,
        ),
    )(g_order, gathered, left)


def on_device(
    grow,
    qpt,
    pair_values,
    pair_scales,
    valence_index,
    conduction_index,
    valence_energy,
    conduction_energy,
    frequencies,
    g_order,
):
    block = pair_values.shape[1] // pair_scales.shape[0]
    pair_count, tile_rows = pair_values.shape
    factor = jnp.repeat(pair_scales, block, axis=0)
    dense = (pair_values.T.astype(jnp.float32) * factor).astype(jnp.bfloat16)
    gathered = gather_rows(dense.reshape(tile_rows * pair_count // LANES, LANES), grow, qpt)
    weights = pair_weights(
        valence_index, conduction_index, valence_energy, conduction_energy, frequencies
    )
    scaled = (weights[:, None, :] * dense.astype(jnp.float32)[None, :, :]).astype(jnp.bfloat16)
    return ordered_product(scaled, gathered, g_order, 16)


def solution(mesh):
    return jax.shard_map(
        functools.partial(on_device, mesh.shape["grow"], mesh.shape["qpt"]),
        mesh=mesh,
        in_specs=(P("qpt", "grow"), P("grow", "qpt"), P("qpt"), P("qpt"), P(), P(), P(), P()),
        out_specs=P(None, ("qpt", "grow"), None),
        check_vma=False,
    )
```

```python
import functools

import jax
import jax.numpy as jnp
from jax import lax
from jax.experimental import pallas as pl
from jax.experimental.pallas import tpu as pltpu
from jax.sharding import PartitionSpec as P

LANES = 128
MESH = pl.DeviceIdType.MESH


def lookup_level(levels, index):
    pair_count = index.shape[1]
    low, high = index & (LANES - 1), index >> 7
    onehot = (lax.broadcasted_iota(jnp.int32, (LANES, pair_count), 0) == low).astype(jnp.float32)
    rows = jnp.dot(
        levels, onehot, precision=lax.Precision.HIGHEST, preferred_element_type=jnp.float32
    )
    hit = lax.broadcasted_iota(jnp.int32, rows.shape, 0) == high
    return jnp.sum(jnp.where(hit, rows, 0.0), axis=0, keepdims=True)


def piece_table(tile_rows, group, across):
    if tile_rows % 128 or tile_rows < 512:
        return [(0, tile_rows * group, False)]
    parts = 4
    part = tile_rows // parts
    if across > 1:
        parts = 6
        part = (tile_rows * 27 // 32) // (parts * 2) * 2
    cuts = [(k * part * group, part * group, False) for k in range(parts)]
    rest = tile_rows - parts * part
    if rest:
        cuts.insert(0, (parts * part * group, rest * group, True))
    return cuts


def gather_kernel(
    deep,
    across,
    pieces,
    x_ref,
    dense_ref,
    valence_ref,
    conduction_ref,
    valence_level_ref,
    conduction_level_ref,
    frequency_ref,
    out_ref,
    left_ref,
    dense,
    left,
    send_sem,
    recv_sem,
    own_sem,
    dense_sem,
    left_sem,
):
    count = len(pieces)
    block_rows = x_ref.shape[0]
    total = deep * across * 2
    q = lax.axis_index("qpt")
    me = lax.axis_index("grow")
    z = me // (2 * across)
    y = (me // 2) % across
    core = me % 2

    def place(zz, yy, cc):
        return (zz * across + yy) * 2 + cc

    beside = place(z, y, 1 - core)
    over = place(z, (across - 1) - y, core)
    up, down = place(z + 1, y, core), place(z - 1, y, core)
    has_up, has_down = z < deep - 1, z > 0

    dense_copy = pltpu.make_async_copy(dense_ref, dense, dense_sem)
    dense_copy.start()
    barrier = pltpu.get_barrier_semaphore()
    pl.semaphore_signal(barrier, inc=1, device_id=(q, beside), device_id_type=MESH)
    if across > 1:
        pl.semaphore_signal(barrier, inc=1, device_id=(q, over), device_id_type=MESH)

    @pl.when(has_up)
    def _():
        pl.semaphore_signal(barrier, inc=1, device_id=(q, up), device_id_type=MESH)

    @pl.when(has_down)
    def _():
        pl.semaphore_signal(barrier, inc=1, device_id=(q, down), device_id_type=MESH)

    pl.semaphore_wait(
        barrier,
        1 + (across > 1) + has_up.astype(jnp.int32) + has_down.astype(jnp.int32),
    )

    def copy(kind, owner, j, target, own):
        first, rows, _ = pieces[j]
        landing = out_ref.at[pl.ds(pl.multiple_of(owner * block_rows + first, 16), rows), :]
        source = x_ref.at[pl.ds(first, rows), :] if own else landing
        slot = owner * count + j
        return pltpu.make_async_remote_copy(
            src_ref=source,
            dst_ref=landing,
            send_sem=send_sem.at[kind * (total * count) + slot],
            recv_sem=recv_sem.at[slot],
            device_id=(q, target),
            device_id_type=MESH,
        )

    def arrive(owner, j):
        copy(0, owner, j, beside, False).wait_recv()

    def pass_on(owner, j, came, same_y, act):
        own = came == 0 and same_y
        early = pieces[j][2]
        along_z = same_y or early
        if along_z and came >= 0:

            @pl.when(has_up)
            def _():
                act(copy(0, owner, j, up, own))

        if along_z and came <= 0:

            @pl.when(has_down)
            def _():
                act(copy(1, owner, j, down, own))

        if across > 1 and same_y and (not early or came == 0):
            act(copy(2, owner, j, over, own))
        act(copy(3, owner, j, beside, own))

    def steps():
        for r in range(1, deep + 1):
            for j in range(count):
                yield r, j

    def visit_half(step, j, same_y, arrived, act):
        yy = y if same_y else (across - 1) - y
        if step == 0:
            owner = place(z, yy, core)
            if arrived and not same_y:
                arrive(owner, j)
            pass_on(owner, j, 0, same_y, act)
            return
        for came in (1, -1):
            near = z - came * step
            inside = (near >= 0) if came == 1 else (near < deep)

            @pl.when(inside)
            def _():
                owner = place(near, yy, core)
                if arrived:
                    arrive(owner, j)
                pass_on(owner, j, came, same_y, act)

    def start(c):
        c.start()

    def sent(c):
        c.wait_send()

    own_copy = pltpu.make_async_copy(
        x_ref, out_ref.at[pl.ds(pl.multiple_of(me * block_rows, 16), block_rows), :], own_sem
    )
    for j in range(count):
        visit_half(0, j, True, True, start)
    own_copy.start()
    dense_copy.wait()
    tile_rows, pair_count = dense.shape
    gap = lookup_level(valence_level_ref[...], valence_ref[...]) - lookup_level(
        conduction_level_ref[...], conduction_ref[...]
    )
    freq_count = left.shape[0]
    weights = [
        2.0 * gap / (gap**2 + frequency_ref[w] ** 2) * float(pair_count) ** (-0.5)
        for w in range(freq_count)
    ]
    chunk = 32

    def scale(i, carry):
        rows = pl.ds(pl.multiple_of(i * chunk, chunk), chunk)
        values = dense[rows, :].astype(jnp.float32)
        for w in range(freq_count):
            left[w, rows, :] = (weights[w] * values).astype(jnp.bfloat16)
        return carry

    lax.fori_loop(0, tile_rows // chunk, scale, 0)
    left_copy = pltpu.make_async_copy(left, left_ref, left_sem)
    left_copy.start()
    for r, j in steps():
        if r < deep:
            visit_half(r, j, True, True, start)
        if across > 1:
            visit_half(r - 1, j, False, True, start)
    for zz in range(deep):
        for yy in range(across):
            for j in range(count):
                arrive(place(zz, yy, 1 - core), j)
    own_copy.wait()
    left_copy.wait()
    for r in range(deep):
        for j in range(count):
            visit_half(r, j, True, False, sent)
            if across > 1:
                visit_half(r, j, False, False, sent)


def gather_rows(dense, pairs, levels, frequencies, total, qpt):
    tile_rows, pair_count = dense.shape
    group = pair_count // LANES
    freq_count = frequencies.shape[0]
    across = max(1, min(4 // max(qpt, 1), total // 2))
    deep = total // (2 * across)
    pieces = piece_table(tile_rows, group, across)
    vmem = pl.BlockSpec(memory_space=pltpu.VMEM)
    left_shape = (freq_count, tile_rows, pair_count)
    return pl.pallas_call(
        functools.partial(gather_kernel, deep, across, pieces),
        out_shape=(
            jax.ShapeDtypeStruct((total * tile_rows * group, LANES), dense.dtype),
            jax.ShapeDtypeStruct(left_shape, dense.dtype),
        ),
        in_specs=[pl.BlockSpec(memory_space=pl.ANY)] * 2
        + [vmem] * 4
        + [pl.BlockSpec(memory_space=pltpu.SMEM)],
        out_specs=(pl.BlockSpec(memory_space=pl.ANY), pl.BlockSpec(memory_space=pl.ANY)),
        scratch_shapes=[
            pltpu.VMEM((tile_rows, pair_count), dense.dtype),
            pltpu.VMEM(left_shape, dense.dtype),
            pltpu.SemaphoreType.DMA((4 * total * len(pieces),)),
            pltpu.SemaphoreType.DMA((total * len(pieces),)),
            pltpu.SemaphoreType.DMA,
            pltpu.SemaphoreType.DMA,
            pltpu.SemaphoreType.DMA,
        ],
        compiler_params=pltpu.CompilerParams(
            collective_id=0, has_side_effects=True, vmem_limit_bytes=56 * 1024 * 1024
        ),
    )(
        dense.reshape(tile_rows * group, LANES),
        dense,
        *[index.reshape(1, pair_count) for index in pairs],
        *[level.reshape(-1, LANES) for level in levels],
        frequencies,
    )


def product_kernel(sources, group, wide, order_ref, src_ref, left_ref, out_ref, natural):
    step = pl.program_id(0)

    @pl.when(step < sources)
    def _():
        pairs = src_ref.shape[0] // (2 * group)

        def place(i, carry):
            rows = src_ref[pl.ds(pl.multiple_of(i * 2 * group, 2 * group), 2 * group), :].astype(
                jnp.float32
            )
            base = step * (2 * pairs) + 2 * i
            for half in range(2):
                g = order_ref[base + half]
                natural[pl.ds(pl.multiple_of(g * group, group), group), :] = rows[
                    half * group : (half + 1) * group
                ]
            return carry

        lax.fori_loop(0, pairs, place, 0, unroll=16)

    @pl.when(step >= sources)
    def _():
        freq_count, tile_rows, pair_count = out_ref.shape[0], out_ref.shape[1], left_ref.shape[1]
        sub = 256
        for n in range(wide // sub):
            first = ((step - sources) * wide + n * sub) * group
            right = jnp.concatenate(
                [
                    natural[pl.ds(first + k, sub, stride=group), :].astype(jnp.bfloat16)
                    for k in range(group)
                ],
                axis=1,
            )
            product = lax.dot_general(
                left_ref[...], right, (((1,), (1,)), ((), ())), preferred_element_type=jnp.float32
            )
            for w in range(freq_count):
                out_ref[w, :, n * sub : (n + 1) * sub] = product[
                    w * tile_rows : (w + 1) * tile_rows
                ]


def ordered_product(left, gathered, g_order, sources):
    freq_count, tile_rows, pair_count = left.shape
    total_cols = g_order.shape[0]
    group = pair_count // LANES
    wide = 1024
    tiles = total_cols // wide
    chunk = gathered.shape[0] // sources
    return pl.pallas_call(
        functools.partial(product_kernel, sources, group, wide),
        out_shape=jax.ShapeDtypeStruct((freq_count, tile_rows, total_cols), jnp.float32),
        grid_spec=pltpu.PrefetchScalarGridSpec(
            num_scalar_prefetch=1,
            grid=(sources + tiles,),
            in_specs=[
                pl.BlockSpec((chunk, LANES), lambda i, order: (jnp.minimum(i, sources - 1), 0)),
                pl.BlockSpec(
                    (freq_count * tile_rows, pair_count),
                    lambda i, order: (0, 0),
                    pipeline_mode=pl.Buffered(1),
                ),
            ],
            out_specs=pl.BlockSpec(
                (freq_count, tile_rows, wide),
                lambda i, order: (0, 0, jnp.maximum(i - sources, 0)),
            ),
            scratch_shapes=[pltpu.VMEM((total_cols * group, LANES), jnp.float32)],
        ),
        compiler_params=pltpu.CompilerParams(
            dimension_semantics=("arbitrary",), vmem_limit_bytes=56 * 1024 * 1024
        ),
        cost_estimate=pl.CostEstimate(
            flops=2 * freq_count * tile_rows * total_cols * pair_count,
            bytes_accessed=freq_count * tile_rows * total_cols * 4,
            transcendentals=0,
        ),
    )(g_order, gathered, left.reshape(freq_count * tile_rows, pair_count))


def on_device(
    grow,
    qpt,
    pair_values,
    pair_scales,
    valence_index,
    conduction_index,
    valence_energy,
    conduction_energy,
    frequencies,
    g_order,
):
    block = pair_values.shape[1] // pair_scales.shape[0]
    pair_count, tile_rows = pair_values.shape
    factor = jnp.repeat(pair_scales, block, axis=0)
    dense = (pair_values.T.astype(jnp.float32) * factor).astype(jnp.bfloat16)
    gathered, left = gather_rows(
        dense,
        (valence_index, conduction_index),
        (valence_energy, conduction_energy),
        frequencies,
        grow,
        qpt,
    )
    return ordered_product(left, gathered, g_order, 8)


def solution(mesh):
    return jax.shard_map(
        functools.partial(on_device, mesh.shape["grow"], mesh.shape["qpt"]),
        mesh=mesh,
        in_specs=(P("qpt", "grow"), P("grow", "qpt"), P("qpt"), P("qpt"), P(), P(), P(), P()),
        out_specs=P(None, ("qpt", "grow"), None),
        check_vma=False,
    )
```

```python
import functools

import jax
import jax.numpy as jnp
from jax import lax
from jax.experimental import pallas as pl
from jax.experimental.pallas import tpu as pltpu
from jax.sharding import PartitionSpec as P

LANES = 128
MESH = pl.DeviceIdType.MESH


def lookup_level(levels, index):
    pair_count = index.shape[1]
    low, high = index & (LANES - 1), index >> 7
    onehot = (lax.broadcasted_iota(jnp.int32, (LANES, pair_count), 0) == low).astype(jnp.float32)
    rows = jnp.dot(
        levels, onehot, precision=lax.Precision.HIGHEST, preferred_element_type=jnp.float32
    )
    hit = lax.broadcasted_iota(jnp.int32, rows.shape, 0) == high
    return jnp.sum(jnp.where(hit, rows, 0.0), axis=0, keepdims=True)


def piece_table(tile_rows, group, across):
    if tile_rows % 128 or tile_rows < 512:
        return [(0, tile_rows * group, False)]
    parts = 4
    part = tile_rows // parts
    if across > 1:
        parts = 6
        part = (tile_rows * 27 // 32) // (parts * 2) * 2
    cuts = [(k * part * group, part * group, False) for k in range(parts)]
    rest = tile_rows - parts * part
    if rest:
        cuts.append((parts * part * group, rest * group, True))
    return cuts


def gather_kernel(
    deep,
    across,
    pieces,
    x_ref,
    dense_ref,
    valence_ref,
    conduction_ref,
    valence_level_ref,
    conduction_level_ref,
    frequency_ref,
    out_ref,
    left_ref,
    dense,
    left,
    send_sem,
    recv_sem,
    own_sem,
    dense_sem,
    left_sem,
):
    count = len(pieces)
    block_rows = x_ref.shape[0]
    total = deep * across * 2
    q = lax.axis_index("qpt")
    me = lax.axis_index("grow")
    z = me // (2 * across)
    y = (me // 2) % across
    core = me % 2

    def place(zz, yy, cc):
        return (zz * across + yy) * 2 + cc

    beside = place(z, y, 1 - core)
    over = place(z, (across - 1) - y, core)
    up, down = place(z + 1, y, core), place(z - 1, y, core)
    has_up, has_down = z < deep - 1, z > 0

    dense_copy = pltpu.make_async_copy(dense_ref, dense, dense_sem)
    dense_copy.start()
    barrier = pltpu.get_barrier_semaphore()
    pl.semaphore_signal(barrier, inc=1, device_id=(q, beside), device_id_type=MESH)
    if across > 1:
        pl.semaphore_signal(barrier, inc=1, device_id=(q, over), device_id_type=MESH)

    @pl.when(has_up)
    def _():
        pl.semaphore_signal(barrier, inc=1, device_id=(q, up), device_id_type=MESH)

    @pl.when(has_down)
    def _():
        pl.semaphore_signal(barrier, inc=1, device_id=(q, down), device_id_type=MESH)

    pl.semaphore_wait(
        barrier,
        1 + (across > 1) + has_up.astype(jnp.int32) + has_down.astype(jnp.int32),
    )

    def copy(kind, owner, j, target, own):
        first, rows, _ = pieces[j]
        landing = out_ref.at[pl.ds(pl.multiple_of(owner * block_rows + first, 16), rows), :]
        source = x_ref.at[pl.ds(first, rows), :] if own else landing
        slot = owner * count + j
        return pltpu.make_async_remote_copy(
            src_ref=source,
            dst_ref=landing,
            send_sem=send_sem.at[kind * (total * count) + slot],
            recv_sem=recv_sem.at[slot],
            device_id=(q, target),
            device_id_type=MESH,
        )

    def arrive(owner, j):
        copy(0, owner, j, beside, False).wait_recv()

    def pass_on(owner, j, came, same_y, act):
        own = came == 0 and same_y
        early = pieces[j][2]
        along_z = same_y or early
        if along_z and came >= 0:

            @pl.when(has_up)
            def _():
                act(copy(0, owner, j, up, own))

        if along_z and came <= 0:

            @pl.when(has_down)
            def _():
                act(copy(1, owner, j, down, own))

        if across > 1 and same_y and (not early or came == 0):
            act(copy(2, owner, j, over, own))
        act(copy(3, owner, j, beside, own))

    def steps():
        for r in range(1, deep + 1):
            for j in range(count):
                yield r, j

    def visit_half(step, j, same_y, arrived, act):
        yy = y if same_y else (across - 1) - y
        if step == 0:
            owner = place(z, yy, core)
            if arrived and not same_y:
                arrive(owner, j)
            pass_on(owner, j, 0, same_y, act)
            return
        for came in (1, -1):
            near = z - came * step
            inside = (near >= 0) if came == 1 else (near < deep)

            @pl.when(inside)
            def _():
                owner = place(near, yy, core)
                if arrived:
                    arrive(owner, j)
                pass_on(owner, j, came, same_y, act)

    def start(c):
        c.start()

    def sent(c):
        c.wait_send()

    own_copy = pltpu.make_async_copy(
        x_ref, out_ref.at[pl.ds(pl.multiple_of(me * block_rows, 16), block_rows), :], own_sem
    )
    for j in (count - 1, *range(count - 1)):
        visit_half(0, j, True, True, start)
    own_copy.start()
    dense_copy.wait()
    tile_rows, pair_count = dense.shape
    gap = lookup_level(valence_level_ref[...], valence_ref[...]) - lookup_level(
        conduction_level_ref[...], conduction_ref[...]
    )
    freq_count = left.shape[0]
    weights = [
        2.0 * gap / (gap**2 + frequency_ref[w] ** 2) * float(pair_count) ** (-0.5)
        for w in range(freq_count)
    ]
    chunk = 32

    def scale(i, carry):
        rows = pl.ds(pl.multiple_of(i * chunk, chunk), chunk)
        values = dense[rows, :].astype(jnp.float32)
        for w in range(freq_count):
            left[w, rows, :] = (weights[w] * values).astype(jnp.bfloat16)
        return carry

    lax.fori_loop(0, tile_rows // chunk, scale, 0)
    left_copy = pltpu.make_async_copy(left, left_ref, left_sem)
    left_copy.start()
    for r, j in steps():
        if r < deep:
            visit_half(r, j, True, True, start)
        if across > 1:
            visit_half(r - 1, j, False, True, start)
    for zz in range(deep):
        for yy in range(across):
            for j in range(count):
                arrive(place(zz, yy, 1 - core), j)
    own_copy.wait()
    left_copy.wait()
    for r in range(deep):
        for j in range(count):
            visit_half(r, j, True, False, sent)
            if across > 1:
                visit_half(r, j, False, False, sent)


def gather_rows(dense, pairs, levels, frequencies, total, qpt):
    tile_rows, pair_count = dense.shape
    group = pair_count // LANES
    freq_count = frequencies.shape[0]
    across = max(1, min(4 // max(qpt, 1), total // 2))
    deep = total // (2 * across)
    pieces = piece_table(tile_rows, group, across)
    vmem = pl.BlockSpec(memory_space=pltpu.VMEM)
    left_shape = (freq_count, tile_rows, pair_count)
    return pl.pallas_call(
        functools.partial(gather_kernel, deep, across, pieces),
        out_shape=(
            jax.ShapeDtypeStruct((total * tile_rows * group, LANES), dense.dtype),
            jax.ShapeDtypeStruct(left_shape, dense.dtype),
        ),
        in_specs=[pl.BlockSpec(memory_space=pl.ANY)] * 2
        + [vmem] * 4
        + [pl.BlockSpec(memory_space=pltpu.SMEM)],
        out_specs=(pl.BlockSpec(memory_space=pl.ANY), pl.BlockSpec(memory_space=pl.ANY)),
        scratch_shapes=[
            pltpu.VMEM((tile_rows, pair_count), dense.dtype),
            pltpu.VMEM(left_shape, dense.dtype),
            pltpu.SemaphoreType.DMA((4 * total * len(pieces),)),
            pltpu.SemaphoreType.DMA((total * len(pieces),)),
            pltpu.SemaphoreType.DMA,
            pltpu.SemaphoreType.DMA,
            pltpu.SemaphoreType.DMA,
        ],
        compiler_params=pltpu.CompilerParams(
            collective_id=0, has_side_effects=True, vmem_limit_bytes=56 * 1024 * 1024
        ),
    )(
        dense.reshape(tile_rows * group, LANES),
        dense,
        *[index.reshape(1, pair_count) for index in pairs],
        *[level.reshape(-1, LANES) for level in levels],
        frequencies,
    )


def product_kernel(sources, group, wide, order_ref, src_ref, left_ref, out_ref, natural):
    step = pl.program_id(0)

    @pl.when(step < sources)
    def _():
        batch = 32
        count = src_ref.shape[0] // group

        def place(i, carry):
            base = step * count + i * batch
            ranks = [order_ref[base + n] * group for n in range(batch)]
            size = batch * group
            rows = src_ref[pl.ds(pl.multiple_of(i * size, size), size), :].astype(jnp.float32)
            for n in range(batch):
                natural[pl.ds(pl.multiple_of(ranks[n], group), group), :] = rows[
                    n * group : (n + 1) * group
                ]
            return carry

        lax.fori_loop(0, count // batch, place, 0)

    @pl.when(step >= sources)
    def _():
        freq_count, tile_rows, pair_count = out_ref.shape[0], out_ref.shape[1], left_ref.shape[1]
        sub = 256
        for n in range(wide // sub):
            first = ((step - sources) * wide + n * sub) * group
            right = jnp.concatenate(
                [
                    natural[pl.ds(first + k, sub, stride=group), :].astype(jnp.bfloat16)
                    for k in range(group)
                ],
                axis=1,
            )
            product = lax.dot_general(
                left_ref[...], right, (((1,), (1,)), ((), ())), preferred_element_type=jnp.float32
            )
            for w in range(freq_count):
                out_ref[w, :, n * sub : (n + 1) * sub] = product[
                    w * tile_rows : (w + 1) * tile_rows
                ]


def ordered_product(left, gathered, g_order, sources):
    freq_count, tile_rows, pair_count = left.shape
    total_cols = g_order.shape[0]
    group = pair_count // LANES
    wide = 1024
    tiles = total_cols // wide
    chunk = gathered.shape[0] // sources
    return pl.pallas_call(
        functools.partial(product_kernel, sources, group, wide),
        out_shape=jax.ShapeDtypeStruct((freq_count, tile_rows, total_cols), jnp.float32),
        grid_spec=pltpu.PrefetchScalarGridSpec(
            num_scalar_prefetch=1,
            grid=(sources + tiles,),
            in_specs=[
                pl.BlockSpec((chunk, LANES), lambda i, order: (jnp.minimum(i, sources - 1), 0)),
                pl.BlockSpec(
                    (freq_count * tile_rows, pair_count),
                    lambda i, order: (0, 0),
                    pipeline_mode=pl.Buffered(1),
                ),
            ],
            out_specs=pl.BlockSpec(
                (freq_count, tile_rows, wide),
                lambda i, order: (0, 0, jnp.maximum(i - sources, 0)),
            ),
            scratch_shapes=[pltpu.VMEM((total_cols * group, LANES), jnp.float32)],
        ),
        compiler_params=pltpu.CompilerParams(
            dimension_semantics=("arbitrary",), vmem_limit_bytes=56 * 1024 * 1024
        ),
        cost_estimate=pl.CostEstimate(
            flops=2 * freq_count * tile_rows * total_cols * pair_count,
            bytes_accessed=freq_count * tile_rows * total_cols * 4,
            transcendentals=0,
        ),
    )(g_order, gathered, left.reshape(freq_count * tile_rows, pair_count))


def on_device(
    grow,
    qpt,
    pair_values,
    pair_scales,
    valence_index,
    conduction_index,
    valence_energy,
    conduction_energy,
    frequencies,
    g_order,
):
    block = pair_values.shape[1] // pair_scales.shape[0]
    pair_count, tile_rows = pair_values.shape
    factor = jnp.repeat(pair_scales, block, axis=0)
    dense = (pair_values.T.astype(jnp.float32) * factor).astype(jnp.bfloat16)
    gathered, left = gather_rows(
        dense,
        (valence_index, conduction_index),
        (valence_energy, conduction_energy),
        frequencies,
        grow,
        qpt,
    )
    return ordered_product(left, gathered, g_order, 8)


def solution(mesh):
    return jax.shard_map(
        functools.partial(on_device, mesh.shape["grow"], mesh.shape["qpt"]),
        mesh=mesh,
        in_specs=(P("qpt", "grow"), P("grow", "qpt"), P("qpt"), P("qpt"), P(), P(), P(), P()),
        out_specs=P(None, ("qpt", "grow"), None),
        check_vma=False,
    )
```

```python
import functools

import jax
import jax.numpy as jnp
from jax import lax
from jax.experimental import pallas as pl
from jax.experimental.pallas import tpu as pltpu
from jax.sharding import PartitionSpec as P

LANES = 128
MESH = pl.DeviceIdType.MESH


def lookup_level(levels, index):
    pair_count = index.shape[1]
    low, high = index & (LANES - 1), index >> 7
    onehot = (lax.broadcasted_iota(jnp.int32, (LANES, pair_count), 0) == low).astype(jnp.float32)
    rows = jnp.dot(
        levels, onehot, precision=lax.Precision.HIGHEST, preferred_element_type=jnp.float32
    )
    hit = lax.broadcasted_iota(jnp.int32, rows.shape, 0) == high
    return jnp.sum(jnp.where(hit, rows, 0.0), axis=0, keepdims=True)


def piece_table(tile_rows, group, across):
    if tile_rows % 128 or tile_rows < 512:
        return [(0, tile_rows * group, False)]
    parts = 4
    part = tile_rows // parts
    if across > 1:
        parts = 6
        part = (tile_rows * 27 // 32) // (parts * 2) * 2
    cuts = [(k * part * group, part * group, False) for k in range(parts)]
    rest = tile_rows - parts * part
    if rest:
        cuts.insert(0, (parts * part * group, rest * group, True))
    return cuts


def gather_kernel(
    deep,
    across,
    pieces,
    x_ref,
    dense_ref,
    valence_ref,
    conduction_ref,
    valence_level_ref,
    conduction_level_ref,
    frequency_ref,
    out_ref,
    left_ref,
    dense,
    left,
    send_sem,
    recv_sem,
    own_sem,
    dense_sem,
    left_sem,
):
    count = len(pieces)
    block_rows = x_ref.shape[0]
    total = deep * across * 2
    q = lax.axis_index("qpt")
    me = lax.axis_index("grow")
    z = me // (2 * across)
    y = (me // 2) % across
    core = me % 2

    def place(zz, yy, cc):
        return (zz * across + yy) * 2 + cc

    beside = place(z, y, 1 - core)
    over = place(z, (across - 1) - y, core)
    up, down = place(z + 1, y, core), place(z - 1, y, core)
    has_up, has_down = z < deep - 1, z > 0

    dense_copy = pltpu.make_async_copy(dense_ref, dense, dense_sem)
    dense_copy.start()
    barrier = pltpu.get_barrier_semaphore()
    pl.semaphore_signal(barrier, inc=1, device_id=(q, beside), device_id_type=MESH)
    if across > 1:
        pl.semaphore_signal(barrier, inc=1, device_id=(q, over), device_id_type=MESH)

    @pl.when(has_up)
    def _():
        pl.semaphore_signal(barrier, inc=1, device_id=(q, up), device_id_type=MESH)

    @pl.when(has_down)
    def _():
        pl.semaphore_signal(barrier, inc=1, device_id=(q, down), device_id_type=MESH)

    pl.semaphore_wait(
        barrier,
        1 + (across > 1) + has_up.astype(jnp.int32) + has_down.astype(jnp.int32),
    )

    def copy(kind, owner, j, target, own):
        first, rows, _ = pieces[j]
        landing = out_ref.at[pl.ds(pl.multiple_of(owner * block_rows + first, 16), rows), :]
        source = x_ref.at[pl.ds(first, rows), :] if own else landing
        slot = owner * count + j
        return pltpu.make_async_remote_copy(
            src_ref=source,
            dst_ref=landing,
            send_sem=send_sem.at[kind * (total * count) + slot],
            recv_sem=recv_sem.at[slot],
            device_id=(q, target),
            device_id_type=MESH,
        )

    def arrive(owner, j):
        copy(0, owner, j, beside, False).wait_recv()

    def pass_on(owner, j, came, same_y, act):
        own = came == 0 and same_y
        early = pieces[j][2]
        along_z = same_y or early
        if along_z and came >= 0:

            @pl.when(has_up)
            def _():
                act(copy(0, owner, j, up, own))

        if along_z and came <= 0:

            @pl.when(has_down)
            def _():
                act(copy(1, owner, j, down, own))

        if across > 1 and same_y and (not early or came == 0):
            act(copy(2, owner, j, over, own))
        act(copy(3, owner, j, beside, own))

    def steps():
        for r in range(1, deep + 1):
            for j in range(count):
                yield r, j

    def visit_half(step, j, same_y, arrived, act):
        yy = y if same_y else (across - 1) - y
        if step == 0:
            owner = place(z, yy, core)
            if arrived and not same_y:
                arrive(owner, j)
            pass_on(owner, j, 0, same_y, act)
            return
        for came in (1, -1):
            near = z - came * step
            inside = (near >= 0) if came == 1 else (near < deep)

            @pl.when(inside)
            def _():
                owner = place(near, yy, core)
                if arrived:
                    arrive(owner, j)
                pass_on(owner, j, came, same_y, act)

    def start(c):
        c.start()

    def sent(c):
        c.wait_send()

    own_copy = pltpu.make_async_copy(
        x_ref, out_ref.at[pl.ds(pl.multiple_of(me * block_rows, 16), block_rows), :], own_sem
    )
    for j in range(count):
        visit_half(0, j, True, True, start)
    own_copy.start()
    dense_copy.wait()
    tile_rows, pair_count = dense.shape
    gap = lookup_level(valence_level_ref[...], valence_ref[...]) - lookup_level(
        conduction_level_ref[...], conduction_ref[...]
    )
    freq_count = left.shape[0]
    weights = [
        2.0 * gap / (gap**2 + frequency_ref[w] ** 2) * float(pair_count) ** (-0.5)
        for w in range(freq_count)
    ]
    chunk = 32

    def scale(i, carry):
        rows = pl.ds(pl.multiple_of(i * chunk, chunk), chunk)
        values = dense[rows, :].astype(jnp.float32)
        for w in range(freq_count):
            left[w, rows, :] = (weights[w] * values).astype(jnp.bfloat16)
        return carry

    lax.fori_loop(0, tile_rows // chunk, scale, 0)
    left_copy = pltpu.make_async_copy(left, left_ref, left_sem)
    left_copy.start()
    for r, j in steps():
        if r < deep:
            visit_half(r, j, True, True, start)
        if across > 1:
            visit_half(r - 1, j, False, True, start)
    for zz in range(deep):
        for yy in range(across):
            for j in range(count):
                arrive(place(zz, yy, 1 - core), j)
    own_copy.wait()
    left_copy.wait()
    for r in range(deep):
        for j in range(count):
            visit_half(r, j, True, False, sent)
            if across > 1:
                visit_half(r, j, False, False, sent)


def gather_rows(dense, pairs, levels, frequencies, total, qpt):
    tile_rows, pair_count = dense.shape
    group = pair_count // LANES
    freq_count = frequencies.shape[0]
    across = max(1, min(4 // max(qpt, 1), total // 2))
    deep = total // (2 * across)
    pieces = piece_table(tile_rows, group, across)
    vmem = pl.BlockSpec(memory_space=pltpu.VMEM)
    left_shape = (freq_count, tile_rows, pair_count)
    return pl.pallas_call(
        functools.partial(gather_kernel, deep, across, pieces),
        out_shape=(
            jax.ShapeDtypeStruct((total * tile_rows * group, LANES), dense.dtype),
            jax.ShapeDtypeStruct(left_shape, dense.dtype),
        ),
        in_specs=[pl.BlockSpec(memory_space=pl.ANY)] * 2
        + [vmem] * 4
        + [pl.BlockSpec(memory_space=pltpu.SMEM)],
        out_specs=(pl.BlockSpec(memory_space=pl.ANY), pl.BlockSpec(memory_space=pl.ANY)),
        scratch_shapes=[
            pltpu.VMEM((tile_rows, pair_count), dense.dtype),
            pltpu.VMEM(left_shape, dense.dtype),
            pltpu.SemaphoreType.DMA((4 * total * len(pieces),)),
            pltpu.SemaphoreType.DMA((total * len(pieces),)),
            pltpu.SemaphoreType.DMA,
            pltpu.SemaphoreType.DMA,
            pltpu.SemaphoreType.DMA,
        ],
        compiler_params=pltpu.CompilerParams(
            collective_id=0, has_side_effects=True, vmem_limit_bytes=56 * 1024 * 1024
        ),
    )(
        dense.reshape(tile_rows * group, LANES),
        dense,
        *[index.reshape(1, pair_count) for index in pairs],
        *[level.reshape(-1, LANES) for level in levels],
        frequencies,
    )


def product_kernel(sources, group, wide, order_ref, src_ref, left_ref, out_ref, natural):
    step = pl.program_id(0)

    @pl.when(step < sources)
    def _():
        batch = 32
        count = src_ref.shape[0] // group

        def place(i, carry):
            base = step * count + i * batch
            ranks = [order_ref[base + n] * group for n in range(batch)]
            size = batch * group
            rows = src_ref[pl.ds(pl.multiple_of(i * size, size), size), :].astype(jnp.float32)
            for n in range(batch):
                natural[pl.ds(pl.multiple_of(ranks[n], group), group), :] = rows[
                    n * group : (n + 1) * group
                ]
            return carry

        lax.fori_loop(0, count // batch, place, 0)

    @pl.when(step >= sources)
    def _():
        freq_count, tile_rows, pair_count = out_ref.shape[0], out_ref.shape[1], left_ref.shape[1]
        sub = 256
        for n in range(wide // sub):
            first = ((step - sources) * wide + n * sub) * group
            right = jnp.concatenate(
                [
                    natural[pl.ds(first + k, sub, stride=group), :].astype(jnp.bfloat16)
                    for k in range(group)
                ],
                axis=1,
            )
            product = lax.dot_general(
                left_ref[...], right, (((1,), (1,)), ((), ())), preferred_element_type=jnp.float32
            )
            for w in range(freq_count):
                out_ref[w, :, n * sub : (n + 1) * sub] = product[
                    w * tile_rows : (w + 1) * tile_rows
                ]


def ordered_product(left, gathered, g_order, sources):
    freq_count, tile_rows, pair_count = left.shape
    total_cols = g_order.shape[0]
    group = pair_count // LANES
    wide = 1024
    tiles = total_cols // wide
    chunk = gathered.shape[0] // sources
    return pl.pallas_call(
        functools.partial(product_kernel, sources, group, wide),
        out_shape=jax.ShapeDtypeStruct((freq_count, tile_rows, total_cols), jnp.float32),
        grid_spec=pltpu.PrefetchScalarGridSpec(
            num_scalar_prefetch=1,
            grid=(sources + tiles,),
            in_specs=[
                pl.BlockSpec((chunk, LANES), lambda i, order: (jnp.minimum(i, sources - 1), 0)),
                pl.BlockSpec(
                    (freq_count * tile_rows, pair_count),
                    lambda i, order: (0, 0),
                    pipeline_mode=pl.Buffered(1),
                ),
            ],
            out_specs=pl.BlockSpec(
                (freq_count, tile_rows, wide),
                lambda i, order: (0, 0, jnp.maximum(i - sources, 0)),
            ),
            scratch_shapes=[pltpu.VMEM((total_cols * group, LANES), jnp.float32)],
        ),
        compiler_params=pltpu.CompilerParams(
            dimension_semantics=("arbitrary",), vmem_limit_bytes=56 * 1024 * 1024
        ),
        cost_estimate=pl.CostEstimate(
            flops=2 * freq_count * tile_rows * total_cols * pair_count,
            bytes_accessed=freq_count * tile_rows * total_cols * 4,
            transcendentals=0,
        ),
    )(g_order, gathered, left.reshape(freq_count * tile_rows, pair_count))


def on_device(
    grow,
    qpt,
    pair_values,
    pair_scales,
    valence_index,
    conduction_index,
    valence_energy,
    conduction_energy,
    frequencies,
    g_order,
):
    block = pair_values.shape[1] // pair_scales.shape[0]
    pair_count, tile_rows = pair_values.shape
    factor = jnp.repeat(pair_scales, block, axis=0)
    dense = (pair_values.T.astype(jnp.float32) * factor).astype(jnp.bfloat16)
    gathered, left = gather_rows(
        dense,
        (valence_index, conduction_index),
        (valence_energy, conduction_energy),
        frequencies,
        grow,
        qpt,
    )
    return ordered_product(left, gathered, g_order, 8)


def solution(mesh):
    return jax.shard_map(
        functools.partial(on_device, mesh.shape["grow"], mesh.shape["qpt"]),
        mesh=mesh,
        in_specs=(P("qpt", "grow"), P("grow", "qpt"), P("qpt"), P("qpt"), P(), P(), P(), P()),
        out_specs=P(None, ("qpt", "grow"), None),
        check_vma=False,
    )
```
